512 devices in a mesh: cam: 32 (over z_hi, x, core), seq: 16 (over y, z_lo).
Axes of the slice: x: 4, y: 8, z: 8 (z_hi: 4, z_lo: 2; z = z_hi * 2 + z_lo), core: 2. Of those that a mesh axis runs over, the one named last changes fastest.
Arguments:
- cross_queries: bfloat16 [32, 4, 512, 2048], P('cam', None, 'seq'), may hold values from -6 to 6
- cross_keys: bfloat16 [32, 4, 512, 2048], P('cam', None, 'seq'), may hold values from -6 to 6
- cross_values: bfloat16 [32, 4, 512, 2048], P('cam', None, 'seq'), may hold values from -6 to 6
- cached_cross: bfloat16 [32, 4, 512, 2048], P('cam', None, 'seq'), may hold values from -6 to 6
- time_queries: bfloat16 [32, 4, 512, 2048], P('cam', None, 'seq'), may hold values from -6 to 6
- time_keys: bfloat16 [32, 4, 512, 2048], P('cam', None, 'seq'), may hold values from -6 to 6
- refresh: int32 [32, 4, 4], P('cam'), may hold values from 0 to 1, as said below
- neighbours: int32 [32, 2], P('cam'), may hold values from 0 to 31, as said below
- view_bias: float32 [3, 16], replicated, may hold values from -1.5 to 1.5
Outputs:
- block_out: bfloat16 [32, 4, 512, 2048], P('cam', None, 'seq')
The draws below stay inside these ranges and needn't reach their ends.
Inputs may be any that keep to these rules, and one draw needn't show every extreme that they name: `refresh`: 1 where the block of 128 positions of that camera and frame is refreshed, 0 where its cached result stands. `neighbours`: row c holds (c - 1) mod 32 and (c + 1) mod 32, in either order.
All inputs are finite; a program needn't handle non-finite values.
Results may differ from the reference program's by a relative error of at most 0.012.
Values may be sent and summed in bfloat16 or wider, within the bound.
A program may use at most 64 MiB of HBM per device.

```python
import math
import jax
import jax.numpy as jnp
from jax import lax

HEADS = 16
HEAD_DIM = 128
FRAMES = 4
BLOCK_ROWS = 128
INNER = 2048
CAMS = 32
POSITIONS = 512


def draw_cross_queries(key, part):
    key = jax.random.fold_in(key, 1)
    shape = (CAMS, FRAMES, POSITIONS, INNER)
    values = jnp.clip(jax.random.normal(key, shape, jnp.float32), -6.0, 6.0)
    return values.astype(jnp.bfloat16)


def draw_cross_keys(key, part):
    key = jax.random.fold_in(key, 2)
    shape = (CAMS, FRAMES, POSITIONS, INNER)
    values = jnp.clip(jax.random.normal(key, shape, jnp.float32), -6.0, 6.0)
    return values.astype(jnp.bfloat16)


def draw_time_queries(key, part):
    key = jax.random.fold_in(key, 3)
    shape = (CAMS, FRAMES, POSITIONS, INNER)
    values = jnp.clip(jax.random.normal(key, shape, jnp.float32), -6.0, 6.0)
    return values.astype(jnp.bfloat16)


def draw_time_keys(key, part):
    key = jax.random.fold_in(key, 4)
    shape = (CAMS, FRAMES, POSITIONS, INNER)
    values = jnp.clip(jax.random.normal(key, shape, jnp.float32), -6.0, 6.0)
    return values.astype(jnp.bfloat16)


def draw_refresh(key, part):
    key = jax.random.fold_in(key, 5)
    level_key, roll_key = jax.random.split(key)
    levels = jax.random.randint(level_key, (CAMS, FRAMES, 1), 0, 5)
    rolls = jax.random.randint(roll_key, (CAMS, FRAMES, POSITIONS // BLOCK_ROWS), 0, 4)
    return (rolls < levels).astype(jnp.int32)


def draw_neighbours(key, part):
    key = jax.random.fold_in(key, 6)
    flips = jax.random.randint(key, (CAMS,), 0, 2)
    camera_ids = jnp.arange(CAMS, dtype=jnp.int32)
    before = (camera_ids + CAMS - 1) % CAMS
    after = (camera_ids + 1) % CAMS
    first = jnp.where(flips == 1, after, before)
    second = jnp.where(flips == 1, before, after)
    return jnp.stack([first, second], axis=1).astype(jnp.int32)


def shard_levels(stream_key, dims, cuts, low, top_value):
    factor_of = 1.0
    for dim, shards_of in cuts:
        draws = jax.random.uniform(jax.random.fold_in(jax.random.fold_in(stream_key, 6), dim), (shards_of,), jnp.float32, low / len(cuts), top_value / len(cuts))
        factor_of = factor_of * jnp.repeat(jnp.exp(draws), dims[dim] // shards_of).reshape((-1,) + (1,) * (len(dims) - 1 - dim))
    return factor_of


def noise(own_key, extent, width, most, shards=(), kind=jnp.bfloat16):
    values = width * jax.random.normal(own_key, extent, jnp.float32)
    if shards:
        values = values * shard_levels(own_key, extent, shards, -0.22, 0.18)
    return jnp.clip(values, -most, most).astype(kind)


def setup_inputs(seed: int = 0) -> dict:
    streams_of = jax.random.split(jax.random.key(seed), 10)
    return {
        "cross_queries": draw_cross_queries(jax.random.fold_in(streams_of[9], 71), 0),
        "cross_keys": draw_cross_keys(jax.random.fold_in(streams_of[9], 71), 0),
        "cross_values": noise(streams_of[2], (CAMS, FRAMES, POSITIONS, INNER), 1.0, 6.0, ((0, 32), (2, 16))),
        "cached_cross": noise(streams_of[3], (CAMS, FRAMES, POSITIONS, INNER), 1.0, 6.0, ((0, 32), (2, 16))),
        "time_queries": draw_time_queries(jax.random.fold_in(streams_of[9], 71), 0),
        "time_keys": draw_time_keys(jax.random.fold_in(streams_of[9], 71), 0),
        "refresh": draw_refresh(jax.random.fold_in(streams_of[9], 71), 0),
        "neighbours": draw_neighbours(jax.random.fold_in(streams_of[9], 71), 0),
        "view_bias": jnp.clip(jax.random.uniform(streams_of[8], (3, HEADS), jnp.float32, -1.5, 1.5), -1.5, 1.5),
    }


def softmax_bf16(scores):
    row_max = lax.optimization_barrier(jnp.max(scores, axis=-1, keepdims=True))
    powers = jnp.exp(scores - row_max)
    return (powers / lax.optimization_barrier(jnp.sum(powers, axis=-1, keepdims=True))).astype(jnp.bfloat16)

def reference(cross_queries, cross_keys, cross_values, cached_cross, time_queries, time_keys, refresh, neighbours, view_bias):
    score_scale = 1.0 / math.sqrt(HEAD_DIM)
    bias_table = jnp.transpose(view_bias).astype(jnp.float32)

    def one_camera(camera):
        camera_ids = jnp.stack([camera.astype(jnp.int32), neighbours[camera, 0].astype(jnp.int32), neighbours[camera, 1].astype(jnp.int32)]).astype(jnp.int32)
        key_sets = cross_keys[camera_ids]
        value_sets = cross_values[camera_ids]

        def one_frame(frame_id):
            query_frame = cross_queries[camera, frame_id].reshape(POSITIONS, HEADS, HEAD_DIM).astype(jnp.float32)
            key_frame = key_sets[:, frame_id].reshape(3, POSITIONS, HEADS, HEAD_DIM).astype(jnp.float32)
            value_frame = value_sets[:, frame_id].reshape(3, POSITIONS, HEADS, HEAD_DIM).astype(jnp.float32)
            scores = jnp.einsum('shd,cthd->hsct', query_frame, key_frame) * score_scale + bias_table[:, None, :, None]
            weights = softmax_bf16(scores.reshape(HEADS, POSITIONS, 3 * POSITIONS)).reshape(HEADS, POSITIONS, 3, POSITIONS)
            cross_out = jnp.einsum('hsct,cthd->shd', weights.astype(jnp.float32), value_frame)
            return cross_out.astype(jnp.bfloat16).reshape(POSITIONS, INNER)
        cross_out = lax.map(one_frame, jnp.arange(FRAMES))
        block_flags = jnp.repeat(refresh[camera], BLOCK_ROWS, axis=1)
        mixed_rows = jnp.where(block_flags[:, :, None] == 1, cross_out, cached_cross[camera])
        shape4 = (FRAMES, POSITIONS, HEADS, HEAD_DIM)
        time_q = time_queries[camera].reshape(shape4).astype(jnp.float32)
        time_k = time_keys[camera].reshape(shape4).astype(jnp.float32)
        time_scores = jnp.einsum('fshd,gshd->shfg', time_q, time_k) * score_scale
        time_weights = softmax_bf16(time_scores)
        result = jnp.einsum('shfg,gshd->fshd', time_weights.astype(jnp.float32), mixed_rows.reshape(shape4).astype(jnp.float32))
        return result.astype(jnp.bfloat16).reshape(FRAMES, POSITIONS, INNER)
    return lax.map(one_camera, jnp.arange(CAMS))
```

```python
import math

import jax
import jax.numpy as jnp
from jax import lax
from jax.experimental import pallas as pl
from jax.experimental.pallas import tpu as pltpu
from jax.sharding import PartitionSpec as P

HEAD_DIM = 128
BLOCK_ROWS = 128
FRAMES = 4
TILE = 128
LOG2E = math.log2(math.e)
MESH = pl.DeviceIdType.MESH


def kernel(
    refresh_ref,
    neighbours_ref,
    bias_ref,
    q_hbm,
    k_hbm,
    v_hbm,
    cached_hbm,
    tq_hbm,
    tk_hbm,
    out_ref,
    kv,
    qb,
    ob,
    mix,
    local3,
    weights,
    in_sem,
    cam_sem,
    back_sem,
    send_sem,
    local_sem,
):
    seq = lax.axis_index("seq")
    cam = lax.axis_index("cam")
    peers = lax.axis_size("seq")
    cams = lax.axis_size("cam")
    rows = q_hbm.shape[2]
    left = lax.rem(cam + cams - 1, cams)
    right = lax.rem(cam + 1, cams)
    blk = lax.div(seq * rows, BLOCK_ROWS)

    barrier = pltpu.get_barrier_semaphore()

    def greet(i, carry):
        pl.semaphore_signal(
            barrier, inc=1, device_id={"seq": lax.rem(seq + i, peers)}, device_id_type=MESH
        )
        return carry

    lax.fori_loop(1, peers, greet, 0)
    for other in (left, right):
        pl.semaphore_signal(barrier, inc=1, device_id={"cam": other}, device_id_type=MESH)
    pl.semaphore_wait(barrier, peers + 1)

    sources = (k_hbm, v_hbm, q_hbm)
    places = (kv.at[0, 0], kv.at[1, 0], qb)

    def head_cols(index):
        return pl.ds(pl.multiple_of(index * HEAD_DIM, HEAD_DIM), HEAD_DIM)

    def my_rows(index):
        return pl.ds(pl.multiple_of(index * rows, rows), rows)

    def scatter(f):
        for a in range(3):

            def send(i, carry):
                peer = lax.rem(seq + i, peers)
                pltpu.make_async_remote_copy(
                    src_ref=sources[a].at[0, f, :, head_cols(peer)],
                    dst_ref=places[a].at[f, my_rows(seq)],
                    send_sem=send_sem.at[a],
                    recv_sem=in_sem.at[a, f],
                    device_id={"seq": peer},
                    device_id_type=MESH,
                ).start()
                return carry

            lax.fori_loop(1, peers, send, 0)
            pltpu.make_async_copy(
                sources[a].at[0, f, :, head_cols(seq)],
                places[a].at[f, my_rows(seq)],
                in_sem.at[a, f],
            ).start()

    def wait_in(a, f):
        pltpu.make_async_copy(places[a].at[f], places[a].at[f], in_sem.at[a, f]).wait()

    def forward(a, f):
        for slot, other in ((1, right), (2, left)):
            pltpu.make_async_remote_copy(
                src_ref=kv.at[a, 0, f],
                dst_ref=kv.at[a, slot, f],
                send_sem=send_sem.at[3],
                recv_sem=cam_sem.at[f],
                device_id={"cam": other},
                device_id_type=MESH,
            ).start()

    scale = LOG2E / math.sqrt(HEAD_DIM)
    left_first = neighbours_ref[0, 0] == left
    bias_own = bias_ref[0, seq] * LOG2E
    bias_a = bias_ref[1, seq] * LOG2E
    bias_b = bias_ref[2, seq] * LOG2E
    biases = (
        bias_own,
        jnp.where(left_first, bias_a, bias_b),
        jnp.where(left_first, bias_b, bias_a),
    )

    def attend(f):
        pltpu.make_async_copy(kv.at[:, 1:3, f], kv.at[:, 1:3, f], cam_sem.at[f]).wait()

        def tile_work(t, carry):
            tile = pl.ds(pl.multiple_of(t * TILE, TILE), TILE)
            query = qb[f, tile]
            scores = [
                lax.dot_general(
                    query,
                    kv[0, j, f],
                    (((1,), (1,)), ((), ())),
                    preferred_element_type=jnp.float32,
                )
                for j in range(3)
            ]
            tops = [
                jnp.max(s, axis=1, keepdims=True) * scale + b for s, b in zip(scores, biases)
            ]
            top = jnp.maximum(jnp.maximum(tops[0], tops[1]), tops[2])
            total = jnp.zeros((TILE, 1), jnp.float32)
            acc = jnp.zeros((TILE, HEAD_DIM), jnp.float32)
            for j in range(3):
                power = jnp.exp2(scores[j] * scale + (biases[j] - top))
                total = total + jnp.sum(power, axis=1, keepdims=True)
                acc = acc + jnp.dot(
                    power.astype(jnp.bfloat16), kv[1, j, f], preferred_element_type=jnp.float32
                )
            ob[f, tile] = (acc / total).astype(jnp.bfloat16)
            return carry

        lax.fori_loop(0, qb.shape[1] // TILE, tile_work, 0)

        def give_back(i, carry):
            peer = lax.rem(seq + i, peers)
            pltpu.make_async_remote_copy(
                src_ref=ob.at[f, my_rows(peer)],
                dst_ref=mix.at[f, :, head_cols(seq)],
                send_sem=send_sem.at[4],
                recv_sem=back_sem.at[f],
                device_id={"seq": peer},
                device_id_type=MESH,
            ).start()
            return carry

        lax.fori_loop(1, peers, give_back, 0)
        pltpu.make_async_copy(
            ob.at[f, my_rows(seq)], mix.at[f, :, head_cols(seq)], back_sem.at[f]
        ).start()

    def time_weights(h, carry):
        cols = head_cols(h)
        keys = [local3[2, g, :, cols].astype(jnp.float32) for g in range(FRAMES)]
        for f in range(FRAMES):
            query = local3[1, f, :, cols].astype(jnp.float32)
            scores = [jnp.sum(query * key, axis=1, keepdims=True) * scale for key in keys]
            top = scores[0]
            for s in scores[1:]:
                top = jnp.maximum(top, s)
            powers = [jnp.exp2(s - top) for s in scores]
            total = powers[0] + powers[1] + powers[2] + powers[3]
            for g in range(FRAMES):
                weights[f, g, :, cols] = jnp.broadcast_to(
                    (powers[g] / total).astype(jnp.bfloat16), (rows, HEAD_DIM)
                )
        return carry

    scatter(0)
    scatter(1)
    own_rows = [
        pltpu.make_async_copy(src.at[0], local3.at[n], local_sem.at[n])
        for n, src in enumerate((cached_hbm, tq_hbm, tk_hbm))
    ]
    for copy in own_rows:
        copy.start()
    for copy in own_rows:
        copy.wait()
    lax.fori_loop(0, peers, time_weights, 0)

    for f in range(FRAMES):
        wait_in(0, f)
        forward(0, f)
        wait_in(1, f)
        forward(1, f)
        wait_in(2, f)
        if f + 2 < FRAMES:
            scatter(f + 2)
        if f > 0:
            attend(f - 1)
    attend(FRAMES - 1)

    for f in range(FRAMES):
        pltpu.make_async_copy(mix.at[f], mix.at[f], back_sem.at[f]).wait()

    flags = [refresh_ref[0, g, blk] == 1 for g in range(FRAMES)]

    def combine(h, carry):
        cols = head_cols(h)
        mixed = [
            jnp.where(flags[g], mix[g, :, cols], local3[0, g, :, cols]).astype(jnp.float32)
            for g in range(FRAMES)
        ]
        for f in range(FRAMES):
            acc = weights[f, 0, :, cols].astype(jnp.float32) * mixed[0]
            for g in range(1, FRAMES):
                acc = acc + weights[f, g, :, cols].astype(jnp.float32) * mixed[g]
            out_ref[0, f, :, cols] = acc.astype(jnp.bfloat16)
        return carry

    lax.fori_loop(0, peers, combine, 0)

    received = qb.shape[1] - rows
    for a in range(3):
        sent = kv.at[0, 0, :, pl.ds(0, received)]
        pltpu.make_async_copy(sent, sent, send_sem.at[a]).wait()
    sent = kv.at[:, 1:3]
    pltpu.make_async_copy(sent, sent, send_sem.at[3]).wait()
    sent = ob.at[:, pl.ds(0, received)]
    pltpu.make_async_copy(sent, sent, send_sem.at[4]).wait()


def local(
    cross_queries,
    cross_keys,
    cross_values,
    cached_cross,
    time_queries,
    time_keys,
    refresh,
    neighbours,
    view_bias,
):
    _, frames, rows, inner = cross_queries.shape
    positions = rows * lax.axis_size("seq")
    dtype = jnp.bfloat16
    smem = pl.BlockSpec(memory_space=pltpu.SMEM)
    hbm = pl.BlockSpec(memory_space=pltpu.HBM)
    return pl.pallas_call(
        kernel,
        out_shape=jax.ShapeDtypeStruct(cross_queries.shape, dtype),
        in_specs=[smem] * 3 + [hbm] * 6,
        out_specs=pl.BlockSpec(memory_space=pltpu.VMEM),
        scratch_shapes=[
            pltpu.VMEM((2, 3, frames, positions, HEAD_DIM), dtype),
            pltpu.VMEM((frames, positions, HEAD_DIM), dtype),
            pltpu.VMEM((frames, positions, HEAD_DIM), dtype),
            pltpu.VMEM((frames, rows, inner), dtype),
            pltpu.VMEM((3, frames, rows, inner), dtype),
            pltpu.VMEM((frames, frames, rows, inner), dtype),
            pltpu.SemaphoreType.DMA((3, frames)),
            pltpu.SemaphoreType.DMA((frames,)),
            pltpu.SemaphoreType.DMA((frames,)),
            pltpu.SemaphoreType.DMA((5,)),
            pltpu.SemaphoreType.DMA((3,)),
        ],
        compiler_params=pltpu.CompilerParams(
            collective_id=0, has_side_effects=True, vmem_limit_bytes=60 << 20
        ),
    )(
        refresh,
        neighbours,
        view_bias,
        cross_queries,
        cross_keys,
        cross_values,
        cached_cross,
        time_queries,
        time_keys,
    )


def solution(mesh):
    in_specs = (
        P("cam", None, "seq", None),
        P("cam", None, "seq", None),
        P("cam", None, "seq", None),
        P("cam", None, "seq", None),
        P("cam", None, "seq", None),
        P("cam", None, "seq", None),
        P("cam", None, None),
        P("cam", None),
        P(),
    )
    out_specs = P("cam", None, "seq", None)
    return jax.shard_map(local, mesh=mesh, in_specs=in_specs, out_specs=out_specs, check_vma=False)
```

```python
import math

import jax
import jax.numpy as jnp
from jax import lax
from jax.experimental import pallas as pl
from jax.experimental.pallas import tpu as pltpu
from jax.sharding import PartitionSpec as P

HEAD_DIM = 128
BLOCK_ROWS = 128
FRAMES = 4
ROW = 8
TILE = 128
LOG2E = math.log2(math.e)
MESH = pl.DeviceIdType.MESH


def kernel(
    refresh_ref,
    neighbours_ref,
    bias_ref,
    q_hbm,
    k_hbm,
    v_hbm,
    cached_hbm,
    tq_hbm,
    tk_hbm,
    out_ref,
    kv,
    qb,
    ob,
    mix,
    local3,
    weights,
    in_sem,
    cam_sem,
    back_sem,
    send_sem,
    local_sem,
    relay_sem,
    relayed,
):
    seq = lax.axis_index("seq")
    cam = lax.axis_index("cam")
    peers = lax.axis_size("seq")
    cams = lax.axis_size("cam")
    rows = q_hbm.shape[2]
    left = lax.rem(cam + cams - 1, cams)
    right = lax.rem(cam + 1, cams)
    blk = lax.div(seq * rows, BLOCK_ROWS)

    place = lax.rem(cam, ROW)
    row = cam - place
    row_before = lax.rem(row + cams - ROW, cams)
    row_after = lax.rem(row + ROW, cams)
    is_first, is_last = place == 0, place == ROW - 1
    hands_right, hands_left = place == 1, place == ROW - 2
    hands_on = hands_right | hands_left
    giver = jnp.where(hands_right, row + ROW - 1, row)
    taker = jnp.where(hands_right, row_after, row_before + ROW - 1)
    helper_out = jnp.where(is_last, row + 1, row + ROW - 2)
    helper_in = jnp.where(is_last, row_after + ROW - 2, row_before + 1)

    barrier = pltpu.get_barrier_semaphore()

    def greet(i, carry):
        pl.semaphore_signal(
            barrier, inc=1, device_id={"seq": lax.rem(seq + i, peers)}, device_id_type=MESH
        )
        return carry

    lax.fori_loop(1, peers, greet, 0)
    for other in (left, right):
        pl.semaphore_signal(barrier, inc=1, device_id={"cam": other}, device_id_type=MESH)

    at_edge = is_first | is_last

    def greet_two(one, two):
        for other in (one, two):
            pl.semaphore_signal(barrier, inc=1, device_id={"cam": other}, device_id_type=MESH)

    @pl.when(hands_on)
    def _():
        greet_two(giver, taker)

    @pl.when(at_edge)
    def _():
        greet_two(helper_out, helper_in)

    pl.semaphore_wait(barrier, peers + 1 + jnp.where(hands_on | at_edge, 2, 0))

    sources = (k_hbm, v_hbm, q_hbm)
    places = (kv.at[0, 0], kv.at[1, 0], qb)

    def head_cols(index):
        return pl.ds(pl.multiple_of(index * HEAD_DIM, HEAD_DIM), HEAD_DIM)

    def my_rows(index):
        return pl.ds(pl.multiple_of(index * rows, rows), rows)

    def scatter(f):
        for a in range(3):

            def send(i, carry):
                peer = lax.rem(seq + i, peers)
                pltpu.make_async_remote_copy(
                    src_ref=sources[a].at[0, f, :, head_cols(peer)],
                    dst_ref=places[a].at[f, my_rows(seq)],
                    send_sem=send_sem.at[a],
                    recv_sem=in_sem.at[a, f],
                    device_id={"seq": peer},
                    device_id_type=MESH,
                ).start()
                return carry

            lax.fori_loop(1, peers, send, 0)
            pltpu.make_async_copy(
                sources[a].at[0, f, :, head_cols(seq)],
                places[a].at[f, my_rows(seq)],
                in_sem.at[a, f],
            ).start()

    def wait_in(a, f):
        pltpu.make_async_copy(places[a].at[f], places[a].at[f], in_sem.at[a, f]).wait()

    def forward(a, f):
        for slot, other, edge in ((1, right, is_last), (2, left, is_first)):

            def send(dst_ref, recv_sem, device):
                pltpu.make_async_remote_copy(
                    src_ref=kv.at[a, 0, f],
                    dst_ref=dst_ref,
                    send_sem=send_sem.at[3],
                    recv_sem=recv_sem,
                    device_id={"cam": device},
                    device_id_type=MESH,
                ).start()

            if a == 1:
                send(kv.at[a, slot, f], cam_sem.at[f], other)
            else:

                @pl.when(edge)
                def _():
                    send(relayed.at[f], relay_sem.at[f], helper_out)

                @pl.when(jnp.logical_not(edge))
                def _():
                    send(kv.at[a, slot, f], cam_sem.at[f], other)

    def hand_on(f):
        for slot, acts in ((1, hands_right), (2, hands_left)):

            @pl.when(acts)
            def _():
                pltpu.make_async_copy(relayed.at[f], relayed.at[f], relay_sem.at[f]).wait()
                pltpu.make_async_remote_copy(
                    src_ref=relayed.at[f],
                    dst_ref=kv.at[0, slot, f],
                    send_sem=send_sem.at[5],
                    recv_sem=cam_sem.at[f],
                    device_id={"cam": taker},
                    device_id_type=MESH,
                ).start()

    scale = LOG2E / math.sqrt(HEAD_DIM)
    left_first = neighbours_ref[0, 0] == left
    bias_own = bias_ref[0, seq] * LOG2E
    bias_a = bias_ref[1, seq] * LOG2E
    bias_b = bias_ref[2, seq] * LOG2E
    biases = (
        bias_own,
        jnp.where(left_first, bias_a, bias_b),
        jnp.where(left_first, bias_b, bias_a),
    )

    def attend(f):
        pltpu.make_async_copy(kv.at[:, 1:3, f], kv.at[:, 1:3, f], cam_sem.at[f]).wait()

        def tile_work(t, carry):
            tile = pl.ds(pl.multiple_of(t * TILE, TILE), TILE)
            query = qb[f, tile]
            scores = [
                lax.dot_general(
                    query,
                    kv[0, j, f],
                    (((1,), (1,)), ((), ())),
                    preferred_element_type=jnp.float32,
                )
                for j in range(3)
            ]
            tops = [
                jnp.max(s, axis=1, keepdims=True) * scale + b for s, b in zip(scores, biases)
            ]
            top = jnp.maximum(jnp.maximum(tops[0], tops[1]), tops[2])
            total = jnp.zeros((TILE, 1), jnp.float32)
            acc = jnp.zeros((TILE, HEAD_DIM), jnp.float32)
            for j in range(3):
                power = jnp.exp2(scores[j] * scale + (biases[j] - top))
                total = total + jnp.sum(power, axis=1, keepdims=True)
                acc = acc + jnp.dot(
                    power.astype(jnp.bfloat16), kv[1, j, f], preferred_element_type=jnp.float32
                )
            ob[f, tile] = (acc / total).astype(jnp.bfloat16)
            return carry

        lax.fori_loop(0, qb.shape[1] // TILE, tile_work, 0)

        def give_back(i, carry):
            peer = lax.rem(seq + i, peers)
            pltpu.make_async_remote_copy(
                src_ref=ob.at[f, my_rows(peer)],
                dst_ref=mix.at[f, :, head_cols(seq)],
                send_sem=send_sem.at[4],
                recv_sem=back_sem.at[f],
                device_id={"seq": peer},
                device_id_type=MESH,
            ).start()
            return carry

        lax.fori_loop(1, peers, give_back, 0)
        pltpu.make_async_copy(
            ob.at[f, my_rows(seq)], mix.at[f, :, head_cols(seq)], back_sem.at[f]
        ).start()

    def time_weights(h, carry):
        cols = head_cols(h)
        keys = [local3[2, g, :, cols].astype(jnp.float32) for g in range(FRAMES)]
        for f in range(FRAMES):
            query = local3[1, f, :, cols].astype(jnp.float32)
            scores = [jnp.sum(query * key, axis=1, keepdims=True) * scale for key in keys]
            top = scores[0]
            for s in scores[1:]:
                top = jnp.maximum(top, s)
            powers = [jnp.exp2(s - top) for s in scores]
            total = powers[0] + powers[1] + powers[2] + powers[3]
            for g in range(FRAMES):
                weights[f, g, :, cols] = jnp.broadcast_to(
                    (powers[g] / total).astype(jnp.bfloat16), (rows, HEAD_DIM)
                )
        return carry

    scatter(0)
    scatter(1)
    own_rows = [
        pltpu.make_async_copy(src.at[0], local3.at[n], local_sem.at[n])
        for n, src in enumerate((cached_hbm, tq_hbm, tk_hbm))
    ]
    for copy in own_rows:
        copy.start()
    for copy in own_rows:
        copy.wait()
    lax.fori_loop(0, peers, time_weights, 0)

    for f in range(FRAMES):
        wait_in(0, f)
        forward(0, f)
        wait_in(1, f)
        forward(1, f)
        hand_on(f)
        wait_in(2, f)
        if f + 2 < FRAMES:
            scatter(f + 2)
        if f > 0:
            attend(f - 1)
    attend(FRAMES - 1)

    for f in range(FRAMES):
        pltpu.make_async_copy(mix.at[f], mix.at[f], back_sem.at[f]).wait()

    flags = [refresh_ref[0, g, blk] == 1 for g in range(FRAMES)]

    def combine(h, carry):
        cols = head_cols(h)
        mixed = [
            jnp.where(flags[g], mix[g, :, cols], local3[0, g, :, cols]).astype(jnp.float32)
            for g in range(FRAMES)
        ]
        for f in range(FRAMES):
            acc = weights[f, 0, :, cols].astype(jnp.float32) * mixed[0]
            for g in range(1, FRAMES):
                acc = acc + weights[f, g, :, cols].astype(jnp.float32) * mixed[g]
            out_ref[0, f, :, cols] = acc.astype(jnp.bfloat16)
        return carry

    lax.fori_loop(0, peers, combine, 0)

    received = qb.shape[1] - rows
    for a in range(3):
        sent = kv.at[0, 0, :, pl.ds(0, received)]
        pltpu.make_async_copy(sent, sent, send_sem.at[a]).wait()
    sent = kv.at[:, 1:3]
    pltpu.make_async_copy(sent, sent, send_sem.at[3]).wait()

    @pl.when(hands_on)
    def _():
        pltpu.make_async_copy(relayed, relayed, send_sem.at[5]).wait()

    sent = ob.at[:, pl.ds(0, received)]
    pltpu.make_async_copy(sent, sent, send_sem.at[4]).wait()


def local(
    cross_queries,
    cross_keys,
    cross_values,
    cached_cross,
    time_queries,
    time_keys,
    refresh,
    neighbours,
    view_bias,
):
    _, frames, rows, inner = cross_queries.shape
    positions = rows * lax.axis_size("seq")
    dtype = jnp.bfloat16
    smem = pl.BlockSpec(memory_space=pltpu.SMEM)
    hbm = pl.BlockSpec(memory_space=pltpu.HBM)
    return pl.pallas_call(
        kernel,
        out_shape=jax.ShapeDtypeStruct(cross_queries.shape, dtype),
        in_specs=[smem] * 3 + [hbm] * 6,
        out_specs=pl.BlockSpec(memory_space=pltpu.VMEM),
        scratch_shapes=[
            pltpu.VMEM((2, 3, frames, positions, HEAD_DIM), dtype),
            pltpu.VMEM((frames, positions, HEAD_DIM), dtype),
            pltpu.VMEM((frames, positions, HEAD_DIM), dtype),
            pltpu.VMEM((frames, rows, inner), dtype),
            pltpu.VMEM((3, frames, rows, inner), dtype),
            pltpu.VMEM((frames, frames, rows, inner), dtype),
            pltpu.SemaphoreType.DMA((3, frames)),
            pltpu.SemaphoreType.DMA((frames,)),
            pltpu.SemaphoreType.DMA((frames,)),
            pltpu.SemaphoreType.DMA((6,)),
            pltpu.SemaphoreType.DMA((3,)),
            pltpu.SemaphoreType.DMA((frames,)),
            pltpu.VMEM((frames, positions, HEAD_DIM), dtype),
        ],
        compiler_params=pltpu.CompilerParams(
            collective_id=0, has_side_effects=True, vmem_limit_bytes=60 << 20
        ),
    )(
        refresh,
        neighbours,
        view_bias,
        cross_queries,
        cross_keys,
        cross_values,
        cached_cross,
        time_queries,
        time_keys,
    )


def solution(mesh):
    in_specs = (
        P("cam", None, "seq", None),
        P("cam", None, "seq", None),
        P("cam", None, "seq", None),
        P("cam", None, "seq", None),
        P("cam", None, "seq", None),
        P("cam", None, "seq", None),
        P("cam", None, None),
        P("cam", None),
        P(),
    )
    out_specs = P("cam", None, "seq", None)
    return jax.shard_map(local, mesh=mesh, in_specs=in_specs, out_specs=out_specs, check_vma=False)
```

```python
import math

import jax
import jax.numpy as jnp
from jax import lax
from jax.experimental import pallas as pl
from jax.experimental.pallas import tpu as pltpu
from jax.sharding import PartitionSpec as P

HEAD_DIM = 128
BLOCK_ROWS = 128
FRAMES = 4
ROW = 8
TILE = 128
LOG2E = math.log2(math.e)
MESH = pl.DeviceIdType.MESH


def kernel(
    refresh_ref,
    neighbours_ref,
    bias_ref,
    q_hbm,
    k_hbm,
    v_hbm,
    cached_hbm,
    tq_hbm,
    tk_hbm,
    out_ref,
    kv,
    qb,
    ob,
    mix,
    local3,
    weights,
    in_sem,
    cam_sem,
    back_sem,
    send_sem,
    local_sem,
    relay_sem,
    relayed,
):
    seq = lax.axis_index("seq")
    cam = lax.axis_index("cam")
    peers = lax.axis_size("seq")
    cams = lax.axis_size("cam")
    rows = q_hbm.shape[2]
    left = lax.rem(cam + cams - 1, cams)
    right = lax.rem(cam + 1, cams)
    blk = lax.div(seq * rows, BLOCK_ROWS)

    place = lax.rem(cam, ROW)
    row = cam - place
    row_before = lax.rem(row + cams - ROW, cams)
    row_after = lax.rem(row + ROW, cams)
    is_first, is_last = place == 0, place == ROW - 1
    is_edge = is_first | is_last
    hands_right = (place == 1) | (place == 2)
    hands_left = (place == ROW - 2) | (place == ROW - 3)
    hands_on = hands_right | hands_left
    handed = jnp.where((place == 1) | (place == ROW - 2), 0, 1)
    giver = jnp.where(hands_right, row + ROW - 1, row)
    taker = jnp.where(hands_right, row_after, row_before + ROW - 1)
    taker_slot = jnp.where(hands_right, 1, 2)

    barrier = pltpu.get_barrier_semaphore()

    def greet(i, carry):
        pl.semaphore_signal(
            barrier, inc=1, device_id={"seq": lax.rem(seq + i, peers)}, device_id_type=MESH
        )
        return carry

    def greet_cam(other):
        pl.semaphore_signal(barrier, inc=1, device_id={"cam": other}, device_id_type=MESH)

    lax.fori_loop(1, peers, greet, 0)

    @pl.when(jnp.logical_not(is_last))
    def _():
        greet_cam(right)

    @pl.when(jnp.logical_not(is_first))
    def _():
        greet_cam(left)

    @pl.when(hands_on)
    def _():
        greet_cam(giver)

    @pl.when(is_first)
    def _():
        greet_cam(row_before + 1)
        greet_cam(row_before + 2)

    @pl.when(is_last)
    def _():
        greet_cam(row_after + ROW - 2)
        greet_cam(row_after + ROW - 3)

    pl.semaphore_wait(barrier, peers + 1 + jnp.where(is_edge | hands_on, 1, 0))

    sources = (k_hbm, v_hbm, q_hbm)
    places = (kv.at[0, 0], kv.at[1, 0], qb)

    def head_cols(index):
        return pl.ds(pl.multiple_of(index * HEAD_DIM, HEAD_DIM), HEAD_DIM)

    def my_rows(index):
        return pl.ds(pl.multiple_of(index * rows, rows), rows)

    def scatter(f, arrays):
        for a in arrays:

            def send(i, carry):
                peer = lax.rem(seq + i, peers)
                pltpu.make_async_remote_copy(
                    src_ref=sources[a].at[0, f, :, head_cols(peer)],
                    dst_ref=places[a].at[f, my_rows(seq)],
                    send_sem=send_sem.at[a],
                    recv_sem=in_sem.at[a, f],
                    device_id={"seq": peer},
                    device_id_type=MESH,
                ).start()
                return carry

            lax.fori_loop(1, peers, send, 0)
            pltpu.make_async_copy(
                sources[a].at[0, f, :, head_cols(seq)],
                places[a].at[f, my_rows(seq)],
                in_sem.at[a, f],
            ).start()

    def wait_in(a, f):
        pltpu.make_async_copy(places[a].at[f], places[a].at[f], in_sem.at[a, f]).wait()

    def forward(a, f):
        for slot, other, edge, helper in (
            (1, right, is_last, row + 1 + a),
            (2, left, is_first, row + ROW - 2 - a),
        ):

            def send(dst_ref, recv_sem, device):
                pltpu.make_async_remote_copy(
                    src_ref=kv.at[a, 0, f],
                    dst_ref=dst_ref,
                    send_sem=send_sem.at[3],
                    recv_sem=recv_sem,
                    device_id={"cam": device},
                    device_id_type=MESH,
                ).start()

            @pl.when(edge)
            def _():
                send(relayed.at[f], relay_sem.at[f], helper)

            @pl.when(jnp.logical_not(edge))
            def _():
                send(kv.at[a, slot, f], cam_sem.at[f], other)

    def hand_on(f):
        @pl.when(hands_on)
        def _():
            pltpu.make_async_copy(relayed.at[f], relayed.at[f], relay_sem.at[f]).wait()
            pltpu.make_async_remote_copy(
                src_ref=relayed.at[f],
                dst_ref=kv.at[handed, taker_slot, f],
                send_sem=send_sem.at[5],
                recv_sem=cam_sem.at[f],
                device_id={"cam": taker},
                device_id_type=MESH,
            ).start()

    scale = LOG2E / math.sqrt(HEAD_DIM)
    left_first = neighbours_ref[0, 0] == left
    bias_own = bias_ref[0, seq] * LOG2E
    bias_a = bias_ref[1, seq] * LOG2E
    bias_b = bias_ref[2, seq] * LOG2E
    biases = (
        bias_own,
        jnp.where(left_first, bias_a, bias_b),
        jnp.where(left_first, bias_b, bias_a),
    )

    def attend(f):
        pltpu.make_async_copy(kv.at[:, 1:3, f], kv.at[:, 1:3, f], cam_sem.at[f]).wait()

        def tile_work(t, carry):
            tile = pl.ds(pl.multiple_of(t * TILE, TILE), TILE)
            query = qb[f, tile]
            scores = [
                lax.dot_general(
                    query,
                    kv[0, j, f],
                    (((1,), (1,)), ((), ())),
                    preferred_element_type=jnp.float32,
                )
                for j in range(3)
            ]
            tops = [
                jnp.max(s, axis=1, keepdims=True) * scale + b for s, b in zip(scores, biases)
            ]
            top = jnp.maximum(jnp.maximum(tops[0], tops[1]), tops[2])
            total = jnp.zeros((TILE, 1), jnp.float32)
            acc = jnp.zeros((TILE, HEAD_DIM), jnp.float32)
            for j in range(3):
                power = jnp.exp2(scores[j] * scale + (biases[j] - top))
                total = total + jnp.sum(power, axis=1, keepdims=True)
                acc = acc + jnp.dot(
                    power.astype(jnp.bfloat16), kv[1, j, f], preferred_element_type=jnp.float32
                )
            ob[f, tile] = (acc / total).astype(jnp.bfloat16)
            return carry

        lax.fori_loop(0, qb.shape[1] // TILE, tile_work, 0)

        def give_back(i, carry):
            peer = lax.rem(seq + i, peers)
            pltpu.make_async_remote_copy(
                src_ref=ob.at[f, my_rows(peer)],
                dst_ref=mix.at[f, :, head_cols(seq)],
                send_sem=send_sem.at[4],
                recv_sem=back_sem.at[f],
                device_id={"seq": peer},
                device_id_type=MESH,
            ).start()
            return carry

        lax.fori_loop(1, peers, give_back, 0)
        pltpu.make_async_copy(
            ob.at[f, my_rows(seq)], mix.at[f, :, head_cols(seq)], back_sem.at[f]
        ).start()

    def time_weights(h, carry):
        cols = head_cols(h)
        keys = [local3[2, g, :, cols].astype(jnp.float32) for g in range(FRAMES)]
        for f in range(FRAMES):
            query = local3[1, f, :, cols].astype(jnp.float32)
            scores = [jnp.sum(query * key, axis=1, keepdims=True) * scale for key in keys]
            top = scores[0]
            for s in scores[1:]:
                top = jnp.maximum(top, s)
            powers = [jnp.exp2(s - top) for s in scores]
            total = powers[0] + powers[1] + powers[2] + powers[3]
            for g in range(FRAMES):
                weights[f, g, :, cols] = jnp.broadcast_to(
                    (powers[g] / total).astype(jnp.bfloat16), (rows, HEAD_DIM)
                )
        return carry

    for f in range(2):
        scatter(f, (0, 1))
    own_rows = [
        pltpu.make_async_copy(src.at[0], local3.at[n], local_sem.at[n])
        for n, src in enumerate((cached_hbm, tq_hbm, tk_hbm))
    ]
    for copy in own_rows:
        copy.start()
    for f in range(FRAMES):
        wait_in(0, f)
        forward(0, f)
        wait_in(1, f)
        forward(1, f)
        hand_on(f)
        if f + 2 < FRAMES:
            scatter(f + 2, (0, 1))
        else:
            scatter(2 * f - 4, (2,))
            scatter(2 * f - 3, (2,))
    for copy in own_rows:
        copy.wait()
    lax.fori_loop(0, peers, time_weights, 0)
    for f in range(FRAMES):
        wait_in(2, f)
        attend(f)

    for f in range(FRAMES):
        pltpu.make_async_copy(mix.at[f], mix.at[f], back_sem.at[f]).wait()

    flags = [refresh_ref[0, g, blk] == 1 for g in range(FRAMES)]

    def combine(h, carry):
        cols = head_cols(h)
        mixed = [
            jnp.where(flags[g], mix[g, :, cols], local3[0, g, :, cols]).astype(jnp.float32)
            for g in range(FRAMES)
        ]
        for f in range(FRAMES):
            acc = weights[f, 0, :, cols].astype(jnp.float32) * mixed[0]
            for g in range(1, FRAMES):
                acc = acc + weights[f, g, :, cols].astype(jnp.float32) * mixed[g]
            out_ref[0, f, :, cols] = acc.astype(jnp.bfloat16)
        return carry

    lax.fori_loop(0, peers, combine, 0)

    received = qb.shape[1] - rows
    for a in range(3):
        sent = kv.at[0, 0, :, pl.ds(0, received)]
        pltpu.make_async_copy(sent, sent, send_sem.at[a]).wait()
    sent = kv.at[:, 1:3]
    pltpu.make_async_copy(sent, sent, send_sem.at[3]).wait()

    @pl.when(hands_on)
    def _():
        pltpu.make_async_copy(relayed, relayed, send_sem.at[5]).wait()

    sent = ob.at[:, pl.ds(0, received)]
    pltpu.make_async_copy(sent, sent, send_sem.at[4]).wait()


def local(
    cross_queries,
    cross_keys,
    cross_values,
    cached_cross,
    time_queries,
    time_keys,
    refresh,
    neighbours,
    view_bias,
):
    _, frames, rows, inner = cross_queries.shape
    positions = rows * lax.axis_size("seq")
    dtype = jnp.bfloat16
    smem = pl.BlockSpec(memory_space=pltpu.SMEM)
    hbm = pl.BlockSpec(memory_space=pltpu.HBM)
    return pl.pallas_call(
        kernel,
        out_shape=jax.ShapeDtypeStruct(cross_queries.shape, dtype),
        in_specs=[smem] * 3 + [hbm] * 6,
        out_specs=pl.BlockSpec(memory_space=pltpu.VMEM),
        scratch_shapes=[
            pltpu.VMEM((2, 3, frames, positions, HEAD_DIM), dtype),
            pltpu.VMEM((frames, positions, HEAD_DIM), dtype),
            pltpu.VMEM((frames, positions, HEAD_DIM), dtype),
            pltpu.VMEM((frames, rows, inner), dtype),
            pltpu.VMEM((3, frames, rows, inner), dtype),
            pltpu.VMEM((frames, frames, rows, inner), dtype),
            pltpu.SemaphoreType.DMA((3, frames)),
            pltpu.SemaphoreType.DMA((frames,)),
            pltpu.SemaphoreType.DMA((frames,)),
            pltpu.SemaphoreType.DMA((6,)),
            pltpu.SemaphoreType.DMA((3,)),
            pltpu.SemaphoreType.DMA((frames,)),
            pltpu.VMEM((frames, positions, HEAD_DIM), dtype),
        ],
        compiler_params=pltpu.CompilerParams(
            collective_id=0, has_side_effects=True, vmem_limit_bytes=60 << 20
        ),
    )(
        refresh,
        neighbours,
        view_bias,
        cross_queries,
        cross_keys,
        cross_values,
        cached_cross,
        time_queries,
        time_keys,
    )


def solution(mesh):
    in_specs = (
        P("cam", None, "seq", None),
        P("cam", None, "seq", None),
        P("cam", None, "seq", None),
        P("cam", None, "seq", None),
        P("cam", None, "seq", None),
        P("cam", None, "seq", None),
        P("cam", None, None),
        P("cam", None),
        P(),
    )
    out_specs = P("cam", None, "seq", None)
    return jax.shard_map(local, mesh=mesh, in_specs=in_specs, out_specs=out_specs, check_vma=False)
```

```python
import math

import jax
import jax.numpy as jnp
from jax import lax
from jax.experimental import pallas as pl
from jax.experimental.pallas import tpu as pltpu
from jax.sharding import PartitionSpec as P

HEAD_DIM = 128
BLOCK_ROWS = 128
FRAMES = 4
ROW = 8
TILE = 256
LOG2E = math.log2(math.e)
MESH = pl.DeviceIdType.MESH


def kernel(
    refresh_ref,
    neighbours_ref,
    bias_ref,
    q_hbm,
    k_hbm,
    v_hbm,
    cached_hbm,
    tq_hbm,
    tk_hbm,
    out_ref,
    kv,
    qb,
    ob,
    mix,
    local3,
    weights,
    in_sem,
    cam_sem,
    back_sem,
    send_sem,
    local_sem,
    relay_sem,
    relayed,
    sums,
):
    seq = lax.axis_index("seq")
    cam = lax.axis_index("cam")
    peers = lax.axis_size("seq")
    cams = lax.axis_size("cam")
    rows = q_hbm.shape[2]
    left = lax.rem(cam + cams - 1, cams)
    right = lax.rem(cam + 1, cams)
    blk = lax.div(seq * rows, BLOCK_ROWS)

    place = lax.rem(cam, ROW)
    row = cam - place
    row_before = lax.rem(row + cams - ROW, cams)
    row_after = lax.rem(row + ROW, cams)
    is_first, is_last = place == 0, place == ROW - 1
    is_edge = is_first | is_last
    hands_right = (place == 1) | (place == 2)
    hands_left = (place == ROW - 2) | (place == ROW - 3)
    hands_on = hands_right | hands_left
    handed = jnp.where((place == 1) | (place == ROW - 2), 0, 1)
    giver = jnp.where(hands_right, row + ROW - 1, row)
    taker = jnp.where(hands_right, row_after, row_before + ROW - 1)
    taker_slot = jnp.where(hands_right, 1, 2)

    barrier = pltpu.get_barrier_semaphore()

    def greet(i, carry):
        pl.semaphore_signal(
            barrier, inc=1, device_id={"seq": lax.rem(seq + i, peers)}, device_id_type=MESH
        )
        return carry

    def greet_cam(other):
        pl.semaphore_signal(barrier, inc=1, device_id={"cam": other}, device_id_type=MESH)

    lax.fori_loop(1, peers, greet, 0)

    @pl.when(jnp.logical_not(is_last))
    def _():
        greet_cam(right)

    @pl.when(jnp.logical_not(is_first))
    def _():
        greet_cam(left)

    @pl.when(hands_on)
    def _():
        greet_cam(giver)

    @pl.when(is_first)
    def _():
        greet_cam(row_before + 1)
        greet_cam(row_before + 2)

    @pl.when(is_last)
    def _():
        greet_cam(row_after + ROW - 2)
        greet_cam(row_after + ROW - 3)

    pl.semaphore_wait(barrier, peers + 1 + jnp.where(is_edge | hands_on, 1, 0))

    sources = (k_hbm, v_hbm, q_hbm)
    places = (kv.at[0, 0], kv.at[1, 0], qb)

    def head_cols(index):
        return pl.ds(pl.multiple_of(index * HEAD_DIM, HEAD_DIM), HEAD_DIM)

    def my_rows(index):
        return pl.ds(pl.multiple_of(index * rows, rows), rows)

    def scatter(f, arrays):
        for a in arrays:

            def send(i, carry):
                peer = lax.rem(seq + i, peers)
                pltpu.make_async_remote_copy(
                    src_ref=sources[a].at[0, f, :, head_cols(peer)],
                    dst_ref=places[a].at[f, my_rows(seq)],
                    send_sem=send_sem.at[a],
                    recv_sem=in_sem.at[a, f],
                    device_id={"seq": peer},
                    device_id_type=MESH,
                ).start()
                return carry

            lax.fori_loop(1, peers, send, 0)
            pltpu.make_async_copy(
                sources[a].at[0, f, :, head_cols(seq)],
                places[a].at[f, my_rows(seq)],
                in_sem.at[a, f],
            ).start()

    def wait_in(a, f):
        pltpu.make_async_copy(places[a].at[f], places[a].at[f], in_sem.at[a, f]).wait()

    def forward(a, f):
        for slot, other, edge, helper in (
            (1, right, is_last, row + 1 + a),
            (2, left, is_first, row + ROW - 2 - a),
        ):

            def send(dst_ref, recv_sem, device):
                pltpu.make_async_remote_copy(
                    src_ref=kv.at[a, 0, f],
                    dst_ref=dst_ref,
                    send_sem=send_sem.at[3],
                    recv_sem=recv_sem,
                    device_id={"cam": device},
                    device_id_type=MESH,
                ).start()

            @pl.when(edge)
            def _():
                send(relayed.at[f], relay_sem.at[f], helper)

            @pl.when(jnp.logical_not(edge))
            def _():
                send(kv.at[a, slot, f], cam_sem.at[f], other)

    def hand_on(f):
        @pl.when(hands_on)
        def _():
            pltpu.make_async_copy(relayed.at[f], relayed.at[f], relay_sem.at[f]).wait()
            pltpu.make_async_remote_copy(
                src_ref=relayed.at[f],
                dst_ref=kv.at[handed, taker_slot, f],
                send_sem=send_sem.at[5],
                recv_sem=cam_sem.at[f],
                device_id={"cam": taker},
                device_id_type=MESH,
            ).start()

    scale = LOG2E / math.sqrt(HEAD_DIM)
    left_first = neighbours_ref[0, 0] == left
    bias_own = bias_ref[0, seq] * LOG2E
    bias_a = bias_ref[1, seq] * LOG2E
    bias_b = bias_ref[2, seq] * LOG2E
    biases = (
        bias_own,
        jnp.where(left_first, bias_a, bias_b),
        jnp.where(left_first, bias_b, bias_a),
    )

    def attend(f):
        pltpu.make_async_copy(kv.at[:, 1:3, f], kv.at[:, 1:3, f], cam_sem.at[f]).wait()

        def tile_work(t, carry):
            tile = pl.ds(pl.multiple_of(t * TILE, TILE), TILE)
            query = qb[f, tile]
            scores = [
                lax.dot_general(
                    query,
                    kv[0, j, f],
                    (((1,), (1,)), ((), ())),
                    preferred_element_type=jnp.float32,
                )
                for j in range(3)
            ]
            tops = [
                jnp.max(s, axis=1, keepdims=True) * scale + b for s, b in zip(scores, biases)
            ]
            top = jnp.maximum(jnp.maximum(tops[0], tops[1]), tops[2])
            total = jnp.zeros((TILE, 1), jnp.float32)
            acc = jnp.zeros((TILE, HEAD_DIM), jnp.float32)
            for j in range(3):
                power = jnp.exp2(scores[j] * scale + (biases[j] - top))
                total = total + jnp.sum(power, axis=1, keepdims=True)
                acc = acc + jnp.dot(
                    power.astype(jnp.bfloat16), kv[1, j, f], preferred_element_type=jnp.float32
                )
            ob[f, tile] = (acc / total).astype(jnp.bfloat16)
            return carry

        def give_back(peer, carry):
            @pl.when(peer != seq)
            def _():
                pltpu.make_async_remote_copy(
                    src_ref=ob.at[f, my_rows(peer)],
                    dst_ref=mix.at[f, :, head_cols(seq)],
                    send_sem=send_sem.at[4],
                    recv_sem=back_sem.at[f],
                    device_id={"seq": peer},
                    device_id_type=MESH,
                ).start()

            @pl.when(peer == seq)
            def _():
                pltpu.make_async_copy(
                    ob.at[f, my_rows(seq)], mix.at[f, :, head_cols(seq)], back_sem.at[f]
                ).start()

            return carry

        def tile_and_send(t, carry):
            tile_work(t, carry)
            lax.fori_loop(t * (TILE // rows), (t + 1) * (TILE // rows), give_back, 0)
            return carry

        lax.fori_loop(0, qb.shape[1] // TILE, tile_and_send, 0)

    def time_weights(h, carry):
        cols = head_cols(h)
        keys = [local3[2, g, :, cols].astype(jnp.float32) for g in range(FRAMES)]
        for f in range(FRAMES):
            query = local3[1, f, :, cols].astype(jnp.float32)
            scores = [jnp.sum(query * key, axis=1, keepdims=True) * scale for key in keys]
            top = scores[0]
            for s in scores[1:]:
                top = jnp.maximum(top, s)
            powers = [jnp.exp2(s - top) for s in scores]
            total = powers[0] + powers[1] + powers[2] + powers[3]
            for g in range(FRAMES):
                weights[f, g, :, cols] = jnp.broadcast_to(
                    (powers[g] / total).astype(jnp.bfloat16), (rows, HEAD_DIM)
                )
        return carry

    for f in range(2):
        scatter(f, (0, 1))
    own_rows = [
        pltpu.make_async_copy(src.at[0], local3.at[n], local_sem.at[n])
        for n, src in enumerate((cached_hbm, tq_hbm, tk_hbm))
    ]
    for copy in own_rows:
        copy.start()
    for f in range(FRAMES):
        wait_in(0, f)
        forward(0, f)
        wait_in(1, f)
        forward(1, f)
        hand_on(f)
        if f + 2 < FRAMES:
            scatter(f + 2, (0, 1))
        else:
            scatter(2 * f - 4, (2,))
            scatter(2 * f - 3, (2,))
    for copy in own_rows:
        copy.wait()
    lax.fori_loop(0, peers, time_weights, 0)
    for f in range(FRAMES):
        wait_in(2, f)
        attend(f)

    flags = [refresh_ref[0, g, blk] == 1 for g in range(FRAMES)]

    def wait_back(g):
        pltpu.make_async_copy(mix.at[g], mix.at[g], back_sem.at[g]).wait()

    def mixed(g, cols):
        return jnp.where(flags[g], mix[g, :, cols], local3[0, g, :, cols]).astype(jnp.float32)

    def term(f, g, cols, value):
        return weights[f, g, :, cols].astype(jnp.float32) * value

    for g in range(FRAMES - 1):
        wait_back(g)

    def combine_first(h, carry):
        cols = head_cols(h)
        values = [mixed(g, cols) for g in range(FRAMES - 1)]
        for f in range(FRAMES):
            acc = term(f, 0, cols, values[0])
            for g in range(1, FRAMES - 1):
                acc = acc + term(f, g, cols, values[g])
            sums[f, :, cols] = acc
        return carry

    lax.fori_loop(0, peers, combine_first, 0)
    wait_back(FRAMES - 1)

    def combine_last(h, carry):
        cols = head_cols(h)
        value = mixed(FRAMES - 1, cols)
        for f in range(FRAMES):
            acc = sums[f, :, cols] + term(f, FRAMES - 1, cols, value)
            out_ref[0, f, :, cols] = acc.astype(jnp.bfloat16)
        return carry

    lax.fori_loop(0, peers, combine_last, 0)

    received = qb.shape[1] - rows
    for a in range(3):
        sent = kv.at[0, 0, :, pl.ds(0, received)]
        pltpu.make_async_copy(sent, sent, send_sem.at[a]).wait()
    sent = kv.at[:, 1:3]
    pltpu.make_async_copy(sent, sent, send_sem.at[3]).wait()

    @pl.when(hands_on)
    def _():
        pltpu.make_async_copy(relayed, relayed, send_sem.at[5]).wait()

    sent = ob.at[:, pl.ds(0, received)]
    pltpu.make_async_copy(sent, sent, send_sem.at[4]).wait()


def local(
    cross_queries,
    cross_keys,
    cross_values,
    cached_cross,
    time_queries,
    time_keys,
    refresh,
    neighbours,
    view_bias,
):
    _, frames, rows, inner = cross_queries.shape
    positions = rows * lax.axis_size("seq")
    dtype = jnp.bfloat16
    smem = pl.BlockSpec(memory_space=pltpu.SMEM)
    hbm = pl.BlockSpec(memory_space=pltpu.HBM)
    return pl.pallas_call(
        kernel,
        out_shape=pltpu.VMEM(cross_queries.shape, dtype),
        in_specs=[smem] * 3 + [hbm] * 6,
        out_specs=pl.BlockSpec(memory_space=pltpu.VMEM),
        scratch_shapes=[
            pltpu.VMEM((2, 3, frames, positions, HEAD_DIM), dtype),
            pltpu.VMEM((frames, positions, HEAD_DIM), dtype),
            pltpu.VMEM((frames, positions, HEAD_DIM), dtype),
            pltpu.VMEM((frames, rows, inner), dtype),
            pltpu.VMEM((3, frames, rows, inner), dtype),
            pltpu.VMEM((frames, frames, rows, inner), dtype),
            pltpu.SemaphoreType.DMA((3, frames)),
            pltpu.SemaphoreType.DMA((frames,)),
            pltpu.SemaphoreType.DMA((frames,)),
            pltpu.SemaphoreType.DMA((6,)),
            pltpu.SemaphoreType.DMA((3,)),
            pltpu.SemaphoreType.DMA((frames,)),
            pltpu.VMEM((frames, positions, HEAD_DIM), dtype),
            pltpu.VMEM((frames, rows, inner), jnp.float32),
        ],
        compiler_params=pltpu.CompilerParams(
            collective_id=0, has_side_effects=True, vmem_limit_bytes=60 << 20
        ),
    )(
        refresh,
        neighbours,
        view_bias,
        pltpu.with_memory_space_constraint(cross_queries, pltpu.HBM),
        pltpu.with_memory_space_constraint(cross_keys, pltpu.HBM),
        pltpu.with_memory_space_constraint(cross_values, pltpu.HBM),
        pltpu.with_memory_space_constraint(cached_cross, pltpu.HBM),
        pltpu.with_memory_space_constraint(time_queries, pltpu.HBM),
        pltpu.with_memory_space_constraint(time_keys, pltpu.HBM),
    )


def solution(mesh):
    in_specs = (
        P("cam", None, "seq", None),
        P("cam", None, "seq", None),
        P("cam", None, "seq", None),
        P("cam", None, "seq", None),
        P("cam", None, "seq", None),
        P("cam", None, "seq", None),
        P("cam", None, None),
        P("cam", None),
        P(),
    )
    out_specs = P("cam", None, "seq", None)
    return jax.shard_map(local, mesh=mesh, in_specs=in_specs, out_specs=out_specs, check_vma=False)
```

```python
import math

import jax
import jax.numpy as jnp
from jax import lax
from jax.experimental import pallas as pl
from jax.experimental.pallas import tpu as pltpu
from jax.sharding import PartitionSpec as P

HEAD_DIM = 128
BLOCK_ROWS = 128
FRAMES = 4
ROW = 8
TILE = 256
LOG2E = math.log2(math.e)
MESH = pl.DeviceIdType.MESH


def kernel(
    refresh_hbm,
    neighbours_hbm,
    bias_hbm,
    q_hbm,
    k_hbm,
    v_hbm,
    cached_hbm,
    tq_hbm,
    tk_hbm,
    out_ref,
    kv,
    qb,
    ob,
    mix,
    local3,
    weights,
    in_sem,
    cam_sem,
    back_sem,
    send_sem,
    local_sem,
    relay_sem,
    relayed,
    refresh_ref,
    neighbours_ref,
    bias_ref,
    sums,
):
    seq = lax.axis_index("seq")
    cam = lax.axis_index("cam")
    peers = lax.axis_size("seq")
    cams = lax.axis_size("cam")
    rows = q_hbm.shape[2]
    left = lax.rem(cam + cams - 1, cams)
    right = lax.rem(cam + 1, cams)
    blk = lax.div(seq * rows, BLOCK_ROWS)

    place = lax.rem(cam, ROW)
    row = cam - place
    row_before = lax.rem(row + cams - ROW, cams)
    row_after = lax.rem(row + ROW, cams)
    is_first, is_last = place == 0, place == ROW - 1
    is_edge = is_first | is_last
    hands_right = (place == 1) | (place == 2)
    hands_left = (place == ROW - 2) | (place == ROW - 3)
    hands_on = hands_right | hands_left
    handed = jnp.where((place == 1) | (place == ROW - 2), 0, 1)
    giver = jnp.where(hands_right, row + ROW - 1, row)
    taker = jnp.where(hands_right, row_after, row_before + ROW - 1)
    taker_slot = jnp.where(hands_right, 1, 2)

    barrier = pltpu.get_barrier_semaphore()

    def greet(i, carry):
        pl.semaphore_signal(
            barrier, inc=1, device_id={"seq": lax.rem(seq + i, peers)}, device_id_type=MESH
        )
        return carry

    def greet_cam(other):
        pl.semaphore_signal(barrier, inc=1, device_id={"cam": other}, device_id_type=MESH)

    lax.fori_loop(1, peers, greet, 0)

    @pl.when(jnp.logical_not(is_last))
    def _():
        greet_cam(right)

    @pl.when(jnp.logical_not(is_first))
    def _():
        greet_cam(left)

    @pl.when(hands_on)
    def _():
        greet_cam(giver)

    @pl.when(is_first)
    def _():
        greet_cam(row_before + 1)
        greet_cam(row_before + 2)

    @pl.when(is_last)
    def _():
        greet_cam(row_after + ROW - 2)
        greet_cam(row_after + ROW - 3)

    pl.semaphore_wait(barrier, peers + 1 + jnp.where(is_edge | hands_on, 1, 0))

    sources = (k_hbm, v_hbm, q_hbm)
    places = (kv.at[0, 0], kv.at[1, 0], qb)

    def head_cols(index):
        return pl.ds(pl.multiple_of(index * HEAD_DIM, HEAD_DIM), HEAD_DIM)

    def my_rows(index):
        return pl.ds(pl.multiple_of(index * rows, rows), rows)

    def scatter(f, arrays):
        for a in arrays:

            def send(i, carry):
                peer = lax.rem(seq + i, peers)
                pltpu.make_async_remote_copy(
                    src_ref=sources[a].at[0, f, :, head_cols(peer)],
                    dst_ref=places[a].at[f, my_rows(seq)],
                    send_sem=send_sem.at[a],
                    recv_sem=in_sem.at[a, f],
                    device_id={"seq": peer},
                    device_id_type=MESH,
                ).start()
                return carry

            lax.fori_loop(1, peers, send, 0)
            pltpu.make_async_copy(
                sources[a].at[0, f, :, head_cols(seq)],
                places[a].at[f, my_rows(seq)],
                in_sem.at[a, f],
            ).start()

    def wait_in(a, f):
        pltpu.make_async_copy(places[a].at[f], places[a].at[f], in_sem.at[a, f]).wait()

    def forward(a, f):
        for slot, other, edge, helper in (
            (1, right, is_last, row + 1 + a),
            (2, left, is_first, row + ROW - 2 - a),
        ):

            def send(dst_ref, recv_sem, device):
                pltpu.make_async_remote_copy(
                    src_ref=kv.at[a, 0, f],
                    dst_ref=dst_ref,
                    send_sem=send_sem.at[3],
                    recv_sem=recv_sem,
                    device_id={"cam": device},
                    device_id_type=MESH,
                ).start()

            @pl.when(edge)
            def _():
                send(relayed.at[f], relay_sem.at[f], helper)

            @pl.when(jnp.logical_not(edge))
            def _():
                send(kv.at[a, slot, f], cam_sem.at[f], other)

    def hand_on(f, kind):
        @pl.when(hands_on & (handed == kind))
        def _():
            pltpu.make_async_copy(relayed.at[f], relayed.at[f], relay_sem.at[f]).wait()
            pltpu.make_async_remote_copy(
                src_ref=relayed.at[f],
                dst_ref=kv.at[handed, taker_slot, f],
                send_sem=send_sem.at[5],
                recv_sem=cam_sem.at[f],
                device_id={"cam": taker},
                device_id_type=MESH,
            ).start()

    def attend(f):
        pltpu.make_async_copy(kv.at[:, 1:3, f], kv.at[:, 1:3, f], cam_sem.at[f]).wait()

        def tile_work(t, carry):
            tile = pl.ds(pl.multiple_of(t * TILE, TILE), TILE)
            query = qb[f, tile]
            scores = [
                lax.dot_general(
                    query,
                    kv[0, j, f],
                    (((1,), (1,)), ((), ())),
                    preferred_element_type=jnp.float32,
                )
                for j in range(3)
            ]
            tops = [
                jnp.max(s, axis=1, keepdims=True) * scale + b for s, b in zip(scores, biases)
            ]
            top = jnp.maximum(jnp.maximum(tops[0], tops[1]), tops[2])
            total = jnp.zeros((TILE, 1), jnp.float32)
            acc = jnp.zeros((TILE, HEAD_DIM), jnp.float32)
            for j in range(3):
                power = jnp.exp2(scores[j] * scale + (biases[j] - top))
                total = total + jnp.sum(power, axis=1, keepdims=True)
                acc = acc + jnp.dot(
                    power.astype(jnp.bfloat16), kv[1, j, f], preferred_element_type=jnp.float32
                )
            ob[f, tile] = (acc / total).astype(jnp.bfloat16)
            return carry

        def give_back(peer, carry):
            @pl.when(peer != seq)
            def _():
                pltpu.make_async_remote_copy(
                    src_ref=ob.at[f, my_rows(peer)],
                    dst_ref=mix.at[f, :, head_cols(seq)],
                    send_sem=send_sem.at[4],
                    recv_sem=back_sem.at[f],
                    device_id={"seq": peer},
                    device_id_type=MESH,
                ).start()

            @pl.when(peer == seq)
            def _():
                pltpu.make_async_copy(
                    ob.at[f, my_rows(seq)], mix.at[f, :, head_cols(seq)], back_sem.at[f]
                ).start()

            return carry

        def tile_and_send(t, carry):
            tile_work(t, carry)
            lax.fori_loop(t * (TILE // rows), (t + 1) * (TILE // rows), give_back, 0)
            return carry

        lax.fori_loop(0, qb.shape[1] // TILE, tile_and_send, 0)

    def time_weights(h, carry):
        cols = head_cols(h)
        keys = [local3[2, g, :, cols].astype(jnp.float32) for g in range(FRAMES)]
        for f in range(FRAMES):
            query = local3[1, f, :, cols].astype(jnp.float32)
            scores = [jnp.sum(query * key, axis=1, keepdims=True) * scale for key in keys]
            top = scores[0]
            for s in scores[1:]:
                top = jnp.maximum(top, s)
            powers = [jnp.exp2(s - top) for s in scores]
            total = powers[0] + powers[1] + powers[2] + powers[3]
            for g in range(FRAMES):
                weights[f, g, :, cols] = jnp.broadcast_to(
                    (powers[g] / total).astype(jnp.bfloat16), (rows, HEAD_DIM)
                )
        return carry

    for f in range(2):
        scatter(f, (0, 1))
    small = [
        pltpu.make_async_copy(src, dst, local_sem.at[3 + n])
        for n, (src, dst) in enumerate(
            ((refresh_hbm, refresh_ref), (neighbours_hbm, neighbours_ref), (bias_hbm, bias_ref))
        )
    ]
    for copy in small:
        copy.start()
    own_rows = [
        pltpu.make_async_copy(src.at[0], local3.at[n], local_sem.at[n])
        for n, src in enumerate((cached_hbm, tq_hbm, tk_hbm))
    ]
    for copy in own_rows:
        copy.start()
    for copy in small:
        copy.wait()

    scale = LOG2E / math.sqrt(HEAD_DIM)
    left_first = neighbours_ref[0, 0] == left
    bias_own = bias_ref[0, seq] * LOG2E
    bias_a = bias_ref[1, seq] * LOG2E
    bias_b = bias_ref[2, seq] * LOG2E
    biases = (
        bias_own,
        jnp.where(left_first, bias_a, bias_b),
        jnp.where(left_first, bias_b, bias_a),
    )

    for f in range(FRAMES):
        wait_in(0, f)
        forward(0, f)
        if f > 0:
            hand_on(f - 1, 1)
        wait_in(1, f)
        forward(1, f)
        hand_on(f, 0)
        if f + 2 < FRAMES:
            scatter(f + 2, (0, 1))
        else:
            scatter(2 * f - 4, (2,))
            scatter(2 * f - 3, (2,))
    hand_on(FRAMES - 1, 1)
    for copy in own_rows:
        copy.wait()
    lax.fori_loop(0, peers, time_weights, 0)
    for f in range(FRAMES):
        wait_in(2, f)
        attend(f)

    flags = [refresh_ref[0, g, blk] == 1 for g in range(FRAMES)]

    def wait_back(g):
        pltpu.make_async_copy(mix.at[g], mix.at[g], back_sem.at[g]).wait()

    def mixed(g, cols):
        return jnp.where(flags[g], mix[g, :, cols], local3[0, g, :, cols]).astype(jnp.float32)

    def term(f, g, cols, value):
        return weights[f, g, :, cols].astype(jnp.float32) * value

    for g in range(FRAMES - 1):
        wait_back(g)

    def combine_first(h, carry):
        cols = head_cols(h)
        values = [mixed(g, cols) for g in range(FRAMES - 1)]
        for f in range(FRAMES):
            acc = term(f, 0, cols, values[0])
            for g in range(1, FRAMES - 1):
                acc = acc + term(f, g, cols, values[g])
            sums[f, :, cols] = acc
        return carry

    lax.fori_loop(0, peers, combine_first, 0)
    wait_back(FRAMES - 1)

    def combine_last(h, carry):
        cols = head_cols(h)
        value = mixed(FRAMES - 1, cols)
        for f in range(FRAMES):
            acc = sums[f, :, cols] + term(f, FRAMES - 1, cols, value)
            out_ref[0, f, :, cols] = acc.astype(jnp.bfloat16)
        return carry

    lax.fori_loop(0, peers, combine_last, 0)

    received = qb.shape[1] - rows
    for a in range(3):
        sent = kv.at[0, 0, :, pl.ds(0, received)]
        pltpu.make_async_copy(sent, sent, send_sem.at[a]).wait()
    sent = kv.at[:, 1:3]
    pltpu.make_async_copy(sent, sent, send_sem.at[3]).wait()

    @pl.when(hands_on)
    def _():
        pltpu.make_async_copy(relayed, relayed, send_sem.at[5]).wait()

    sent = ob.at[:, pl.ds(0, received)]
    pltpu.make_async_copy(sent, sent, send_sem.at[4]).wait()


def local(
    cross_queries,
    cross_keys,
    cross_values,
    cached_cross,
    time_queries,
    time_keys,
    refresh,
    neighbours,
    view_bias,
):
    _, frames, rows, inner = cross_queries.shape
    positions = rows * lax.axis_size("seq")
    dtype = jnp.bfloat16
    hbm = pl.BlockSpec(memory_space=pltpu.HBM)
    return pl.pallas_call(
        kernel,
        out_shape=pltpu.VMEM(cross_queries.shape, dtype),
        in_specs=[hbm] * 9,
        out_specs=pl.BlockSpec(memory_space=pltpu.VMEM),
        scratch_shapes=[
            pltpu.VMEM((2, 3, frames, positions, HEAD_DIM), dtype),
            pltpu.VMEM((frames, positions, HEAD_DIM), dtype),
            pltpu.VMEM((frames, positions, HEAD_DIM), dtype),
            pltpu.VMEM((frames, rows, inner), dtype),
            pltpu.VMEM((3, frames, rows, inner), dtype),
            pltpu.VMEM((frames, frames, rows, inner), dtype),
            pltpu.SemaphoreType.DMA((3, frames)),
            pltpu.SemaphoreType.DMA((frames,)),
            pltpu.SemaphoreType.DMA((frames,)),
            pltpu.SemaphoreType.DMA((6,)),
            pltpu.SemaphoreType.DMA((6,)),
            pltpu.SemaphoreType.DMA((frames,)),
            pltpu.VMEM((frames, positions, HEAD_DIM), dtype),
            pltpu.SMEM(refresh.shape, refresh.dtype),
            pltpu.SMEM(neighbours.shape, neighbours.dtype),
            pltpu.SMEM(view_bias.shape, view_bias.dtype),
            pltpu.VMEM((frames, rows, inner), jnp.float32),
        ],
        compiler_params=pltpu.CompilerParams(
            collective_id=0, has_side_effects=True, vmem_limit_bytes=60 << 20
        ),
    )(
        pltpu.with_memory_space_constraint(refresh, pltpu.HBM),
        pltpu.with_memory_space_constraint(neighbours, pltpu.HBM),
        pltpu.with_memory_space_constraint(view_bias, pltpu.HBM),
        pltpu.with_memory_space_constraint(cross_queries, pltpu.HBM),
        pltpu.with_memory_space_constraint(cross_keys, pltpu.HBM),
        pltpu.with_memory_space_constraint(cross_values, pltpu.HBM),
        pltpu.with_memory_space_constraint(cached_cross, pltpu.HBM),
        pltpu.with_memory_space_constraint(time_queries, pltpu.HBM),
        pltpu.with_memory_space_constraint(time_keys, pltpu.HBM),
    )


def solution(mesh):
    in_specs = (
        P("cam", None, "seq", None),
        P("cam", None, "seq", None),
        P("cam", None, "seq", None),
        P("cam", None, "seq", None),
        P("cam", None, "seq", None),
        P("cam", None, "seq", None),
        P("cam", None, None),
        P("cam", None),
        P(),
    )
    out_specs = P("cam", None, "seq", None)
    return jax.shard_map(local, mesh=mesh, in_specs=in_specs, out_specs=out_specs, check_vma=False)
```
